32 devices in a mesh: aux: 8 (over y, x, core), sec: 4 (over z).
Axes of the slice: x: 2, y: 2, z: 4, core: 2. Of those that a mesh axis runs over, the one named last changes fastest.
Arguments:
- wavefunction: bfloat16 [4096, 2048], P('sec'), may hold values from -6 to 6
- dressed_ops: bfloat16 [4096, 5120], P('sec', 'aux'), may hold values from -0.09375 to 0.09375
- site_tensor: bfloat16 [4096, 4096], P('sec'), may hold values from -6 to 6
- old_sector: int32 [4096], P('sec'), may hold values from 0 to 15, never falling along the last dimension, each value on 1 to 1024 neighbouring positions
- new_sector: int32 [4096], replicated, may hold values from 0 to 15, never falling along the last dimension, each value on 1 to 1024 neighbouring positions
Outputs:
- sigma: bfloat16 [4096, 2048], P(('sec', 'aux'))
- rotated_ops: bfloat16 [4096, 5120], P('sec', 'aux')
The draws below stay inside these ranges and needn't reach their ends.
All inputs are finite; a program needn't handle non-finite values.
Results may differ from the reference program's by a relative error of at most 0.0034.
Values may be sent and summed in bfloat16 or wider, within the bound.
A program may use at most 128 MiB of HBM per device.

```python
import math
import jax
import jax.numpy as jnp
import numpy as np
from jax import lax

NORB = 80
NAUX = 64
M = 4096
R = 2048
SECT = 16
SMOST = 1024


def steps_of(own_key, dims, split, smallest, high):
    factor_of = 1.0
    for position, blocks in split:
        heights = jax.random.uniform(jax.random.fold_in(jax.random.fold_in(own_key, 6), position), (blocks,), jnp.float32, smallest / len(split), high / len(split))
        factor_of = factor_of * jnp.repeat(jnp.exp(heights), dims[position] // blocks).reshape((-1,) + (1,) * (len(dims) - 1 - position))
    return factor_of


def length_profile(number_of, total, reach, slope):
    loads = [(1 << 20) // math.isqrt(rank ** slope) + 1 for rank in range(2, number_of + 1)]
    spare, counts = total - reach - (number_of - 1), [1] * (number_of - 1)
    while spare > 0:
        movable = [i for i in range(number_of - 1) if counts[i] < reach]
        whole, left = sum([loads[i] for i in movable]), spare
        for i in movable:
            addition = min(reach - counts[i], max(1, left * loads[i] // whole), spare)
            counts[i] = counts[i] + addition
            spare = spare - addition
    return np.array([reach] + counts)


def uneven(key, count, total, most, lean):
    if count == 2:
        one = jax.random.randint(key, (), max(1, total - most), min(most, total - 1) + 1)
        return jnp.stack([one, total - one])
    lengths = jnp.asarray(length_profile(count, total, most, lean), jnp.int32)
    twos = (count - 1) // 2
    source_of, receiver = lengths[1:1 + 2 * twos:2], lengths[2:2 + 2 * twos:2]
    room = jnp.minimum(source_of - 1, most - receiver)
    shifted = jax.random.randint(jax.random.fold_in(key, 1), (twos,), 0, 1 << 20) % (room + 1)
    lengths = lengths.at[1:1 + 2 * twos:2].set(source_of - shifted).at[2:2 + 2 * twos:2].set(receiver + shifted)
    return lengths[jax.random.permutation(jax.random.fold_in(key, 2), count)]


def noise(rng, extent, scale, reach, cuts=(), kind=jnp.bfloat16):
    loudness = steps_of(rng, extent, cuts, -0.22, 0.18) if cuts else 1.0
    result = jax.random.normal(rng, extent, jnp.float32) * scale * loudness
    return jnp.minimum(jnp.maximum(result, -reach), reach).astype(kind)


def setup_inputs(seed: int = 0) -> dict:
    arg_keys = jax.random.split(jax.random.key(seed), 6)
    wavefunction = noise(arg_keys[0], (M, R), 1.0, 6.0, ((0, 4),))
    dressed_ops = noise(arg_keys[1], (M, NAUX * NORB), M ** -0.5, 0.09375, ((0, 4), (1, 8)))
    site_tensor = noise(arg_keys[2], (M, M), 1.0, 6.0, ((0, 4),))
    old_sector = jnp.searchsorted(jnp.cumsum(uneven(arg_keys[3], SECT, M, SMOST, 2)), jnp.arange(M), side="right").astype(jnp.int32)
    new_sector = jnp.searchsorted(jnp.cumsum(uneven(arg_keys[4], SECT, M, SMOST, 2)), jnp.arange(M), side="right").astype(jnp.int32)
    return dict(wavefunction=wavefunction, dressed_ops=dressed_ops, site_tensor=site_tensor, old_sector=old_sector, new_sector=new_sector)


def reference(wavefunction, dressed_ops, site_tensor, old_sector, new_sector):
    images = lax.dot_general(dressed_ops, wavefunction, (((0,), (0,)), ((), ())), preferred_element_type=jnp.float32)
    images = images.astype(jnp.bfloat16)
    sigma = jnp.dot(dressed_ops, images, preferred_element_type=jnp.float32).astype(jnp.bfloat16)
    offset = new_sector[None, :] - old_sector[:, None]
    allowed = (offset >= 0) & (offset <= 2)
    site_blocks = jnp.where(allowed, site_tensor, jnp.zeros_like(site_tensor))
    rotated = lax.dot_general(site_blocks, dressed_ops, (((0,), (0,)), ((), ())), preferred_element_type=jnp.float32)
    return sigma, rotated.astype(jnp.bfloat16)
```

```python
import functools

import jax
import jax.numpy as jnp
from jax import lax
from jax.experimental import pallas as pl
from jax.experimental.pallas import tpu as pltpu
from jax.sharding import PartitionSpec as P

MESH = pl.DeviceIdType.MESH
CHUNKS = 4


def tdot(a, b):
    return lax.dot_general(a, b, (((0,), (0,)), ((), ())), preferred_element_type=jnp.float32)


def kernel(
    nz, na, w_ref, d_ref, s_ref, old_ref, new_ref, sig_ref, rot_ref,
    wf, sf, df, sm, acc, img, rotacc, keep, msend, mrecv, ssend, srecv, tmp,
    loc, z_s, z_r, dr_s, dl_s, d_r, p_s, p_r, m_s, m_r, x_s, x_r, y_s, y_r,
):
    nc = na // 2
    z = lax.axis_index("sec")
    a = lax.axis_index("aux")
    c = lax.rem(a, 2)
    q = a // 2
    mate = a + 1 - 2 * c
    local = d_ref.shape[0]
    rows = local // na
    width = sf.shape[2]
    cols = w_ref.shape[1]
    step = cols // CHUNKS

    def peer(k):
        return lax.rem(a + 2 * k, na)

    def back(k):
        return lax.rem(a + na - 2 * k, na)

    def part(b):
        return pl.ds(pl.multiple_of(b * rows, rows), rows)

    def block(t):
        return pl.ds(pl.multiple_of(t * width, width), width)

    mine = part(a)

    loads = [
        pltpu.make_async_copy(s_ref.at[mine], sm, loc.at[0]),
        pltpu.make_async_copy(d_ref, df.at[z], loc.at[1]),
        pltpu.make_async_copy(w_ref, wf.at[z], loc.at[2]),
        pltpu.make_async_copy(s_ref.at[:, block(z)], sf.at[z], loc.at[3]),
    ]
    for load in loads:
        load.start()

    barrier = pltpu.get_barrier_semaphore()
    for k in range(1, nz):
        pl.semaphore_signal(barrier, inc=1, device_id={"sec": lax.rem(z + k, nz)}, device_id_type=MESH)
    for k in range(1, nc):
        pl.semaphore_signal(barrier, inc=1, device_id={"aux": peer(k)}, device_id_type=MESH)
    pl.semaphore_signal(barrier, inc=1, device_id={"aux": mate}, device_id_type=MESH)
    pl.semaphore_wait(barrier, nz - 1 + nc - 1 + 1)

    def remote(src, dst, send, recv, where):
        return pltpu.make_async_remote_copy(
            src_ref=src, dst_ref=dst, send_sem=send, recv_sem=recv, device_id=where, device_id_type=MESH
        )

    def z_copy(kind, k):
        t = lax.rem(z + k, nz)
        if kind == 0:
            src, dst = w_ref.at[mine], wf.at[z, mine]
        else:
            src, dst = sm.at[:, block(t)], sf.at[z, mine]
        return remote(src, dst, z_s.at[kind, k], z_r.at[kind, k], {"sec": t})

    full = (wf, sf)

    def z_arrived(kind, k):
        p = lax.rem(z + nz - k, nz)
        ref = full[kind].at[p, mine]
        remote(ref, ref, z_s.at[kind, k], z_r.at[kind, k], {"sec": p}).wait_recv()

    def p_copy(kind, j, k):
        ref = full[kind].at[lax.rem(z + nz - j, nz), mine]
        return remote(ref, ref, p_s.at[kind, j, k], p_r.at[kind, j, k], {"aux": peer(k)})

    def p_arrived(kind, j, k):
        ref = full[kind].at[lax.rem(z + nz - j, nz), part(back(k))]
        remote(ref, ref, p_s.at[kind, j, k], p_r.at[kind, j, k], {"aux": back(k)}).wait_recv()

    def m_copy(kind, j, k):
        ref = full[kind].at[lax.rem(z + nz - j, nz), part(back(k))]
        return remote(ref, ref, m_s.at[kind, j, k], m_r.at[kind, j, k], {"aux": mate})

    def m_arrived(kind, j, k):
        theirs = lax.rem(mate + na - 2 * k, na)
        ref = full[kind].at[lax.rem(z + nz - j, nz), part(theirs)]
        remote(ref, ref, m_s.at[kind, j, k], m_r.at[kind, j, k], {"aux": mate}).wait_recv()

    def spread(kind, j):
        z_arrived(kind, j)
        for k in range(1, nc):
            p_copy(kind, j, k).start()
        m_copy(kind, j, 0).start()

    def relay(kind, j):
        for k in range(1, nc):
            p_arrived(kind, j, k)
            m_copy(kind, j, k).start()

    def landed(kind, j):
        for k in range(nc):
            m_arrived(kind, j, k)

    def d_right(p):
        return remote(df.at[p], df.at[p], dr_s.at[p], d_r.at[p], {"sec": z + 1})

    def d_left(p):
        return remote(df.at[p], df.at[p], dl_s.at[p], d_r.at[p], {"sec": z - 1})

    def d_step(distance):
        @pl.when(z - distance >= 0)
        def _():
            p = z - distance
            remote(df.at[p], df.at[p], dr_s.at[p], d_r.at[p], {"sec": z - 1}).wait_recv()

            @pl.when(z < nz - 1)
            def _():
                d_right(p).start()

        @pl.when(z + distance < nz)
        def _():
            p = z + distance
            remote(df.at[p], df.at[p], dl_s.at[p], d_r.at[p], {"sec": z + 1}).wait_recv()

            @pl.when(z > 0)
            def _():
                d_left(p).start()

    for k in range(1, nz):
        z_copy(0, k).start()
    loads[1].wait()

    @pl.when(z < nz - 1)
    def _():
        d_right(z).start()

    @pl.when(z > 0)
    def _():
        d_left(z).start()

    loads[0].wait()
    for t in range(nz):
        band = pl.ds(t * width, width)
        offset = new_ref[:, band] - old_ref[mine, :]
        allowed = (offset >= 0) & (offset <= 2)
        sm[:, band] = jnp.where(allowed, sm[:, band].astype(jnp.float32), 0.0).astype(jnp.bfloat16)
    for k in range(1, nz):
        z_copy(1, k).start()

    loads[3].wait()

    @pl.loop(0, local // 128)
    def _(i):
        r = pl.ds(pl.multiple_of(i * 128, 128), 128)
        offset = new_ref[:, block(z)] - old_ref[r, :]
        allowed = (offset >= 0) & (offset <= 2)
        sf[z, r, :] = jnp.where(allowed, sf[z, r, :].astype(jnp.float32), 0.0).astype(jnp.bfloat16)

    loads[2].wait()

    def add_images(p, first):
        @pl.loop(0, cols // 512)
        def _(i):
            r = pl.ds(pl.multiple_of(i * 512, 512), 512)
            term = tdot(df[p], wf[p, :, r])
            acc[:, r] = term if first else acc[:, r] + term

    def add_rotated(p, first):
        @pl.loop(0, width // 256)
        def _(i):
            r = pl.ds(pl.multiple_of(i * 256, 256), 256)
            term = tdot(sf[p, :, r], df[p])
            rotacc[r, :] = term if first else rotacc[r, :] + term

    add_images(z, True)
    add_rotated(z, True)

    near = [1, nz - 1] + list(range(2, nz - 1))
    for j in near:
        spread(0, j)
    d_step(1)
    for j in near:
        spread(1, j)
    for j in near:
        relay(0, j)
    for d in range(2, nz):
        d_step(d)
        if d == 2:
            for j in near:
                relay(1, j)
            for j in near:
                landed(0, j)

    for j in range(1, nz):
        add_images(lax.rem(z + nz - j, nz), False)

    @pl.loop(0, CHUNKS)
    def _(i):
        r = pl.ds(pl.multiple_of(i * step, step), step)
        img[:, r] = acc[:, r].astype(jnp.bfloat16)

    def x_copy(i):
        r = pl.ds(i * step, step)
        return remote(msend.at[:, :, r], mrecv.at[:, :, r], x_s.at[i], x_r.at[i], {"aux": mate})

    def y_copy(i, k):
        r = pl.ds(i * step, step)
        return remote(ssend.at[k, :, r], srecv.at[k, :, r], y_s.at[i, k], y_r.at[i, k], {"aux": peer(k)})

    def terms(i):
        r = pl.ds(i * step, step)

        @pl.loop(0, nc)
        def _(b):
            pair = pl.ds(pl.multiple_of(b * 2 * rows, 2 * rows), 2 * rows)
            tmp[...] = jnp.dot(df[z, pair, :], img[:, r], preferred_element_type=jnp.float32)
            keep[b, :, r] = tmp[part(c), :]
            msend[b, :, r] = tmp[part(1 - c), :].astype(jnp.bfloat16)

        x_copy(i).start()

    def combine(i):
        r = pl.ds(i * step, step)
        x_copy(i).wait_recv()
        for k in range(1, nc):
            b = lax.rem(q + k, nc)
            ssend[k, :, r] = (keep[b, :, r] + mrecv[b, :, r].astype(jnp.float32)).astype(jnp.bfloat16)
            y_copy(i, k).start()

    for i in range(CHUNKS):
        terms(i)
        if i > 0:
            combine(i - 1)
    combine(CHUNKS - 1)

    for j in near:
        landed(1, j)
    for j in range(1, nz):
        add_rotated(lax.rem(z + nz - j, nz), False)
    rot_ref[...] = rotacc[...].astype(jnp.bfloat16)

    for i in range(CHUNKS):
        r = pl.ds(i * step, step)
        total = keep[q, :, r] + mrecv[q, :, r].astype(jnp.float32)
        for k in range(1, nc):
            y_copy(i, k).wait_recv()
            total = total + srecv[k, :, r].astype(jnp.float32)
        sig_ref[:, r] = total.astype(jnp.bfloat16)

    for kind in range(2):
        for j in range(1, nz):
            z_copy(kind, j).wait_send()
            for k in range(1, nc):
                p_copy(kind, j, k).wait_send()
            for k in range(nc):
                m_copy(kind, j, k).wait_send()
    for p in range(nz):
        @pl.when((p <= z) & (z < nz - 1))
        def _():
            d_right(p).wait_send()

        @pl.when((p >= z) & (z > 0))
        def _():
            d_left(p).wait_send()
    for i in range(CHUNKS):
        x_copy(i).wait_send()
        for k in range(1, nc):
            y_copy(i, k).wait_send()


def body(nz, na, wavefunction, dressed_ops, site_tensor, old_sector, new_sector):
    local, depth = dressed_ops.shape
    cols = wavefunction.shape[1]
    width = site_tensor.shape[1] // nz
    nc, rows = na // 2, local // na
    bf, f4 = jnp.bfloat16, jnp.float32
    dma = pltpu.SemaphoreType.DMA
    vmem = pl.BlockSpec(memory_space=pltpu.VMEM)
    hbm = pl.BlockSpec(memory_space=pl.ANY)
    return pl.pallas_call(
        functools.partial(kernel, nz, na),
        out_shape=(
            jax.ShapeDtypeStruct((rows, cols), bf),
            jax.ShapeDtypeStruct((width, depth), bf),
        ),
        in_specs=[hbm, hbm, hbm, vmem, vmem],
        out_specs=(vmem, vmem),
        scratch_shapes=[
            pltpu.VMEM((nz, local, cols), bf),
            pltpu.VMEM((nz, local, width), bf),
            pltpu.VMEM((nz, local, depth), bf),
            pltpu.VMEM((rows, nz * width), bf),
            pltpu.VMEM((depth, cols), f4),
            pltpu.VMEM((depth, cols), bf),
            pltpu.VMEM((width, depth), f4),
            pltpu.VMEM((nc, rows, cols), f4),
            pltpu.VMEM((nc, rows, cols), bf),
            pltpu.VMEM((nc, rows, cols), bf),
            pltpu.VMEM((nc, rows, cols), bf),
            pltpu.VMEM((nc, rows, cols), bf),
            pltpu.VMEM((2 * rows, cols // CHUNKS), f4),
            dma((4,)),
            dma((2, nz)),
            dma((2, nz)),
            dma((nz,)),
            dma((nz,)),
            dma((nz,)),
            dma((2, nz, nc)),
            dma((2, nz, nc)),
            dma((2, nz, nc)),
            dma((2, nz, nc)),
            dma((CHUNKS,)),
            dma((CHUNKS,)),
            dma((CHUNKS, nc)),
            dma((CHUNKS, nc)),
        ],
        compiler_params=pltpu.CompilerParams(
            collective_id=0, has_side_effects=True, vmem_limit_bytes=64 * 1024 * 1024
        ),
    )(wavefunction, dressed_ops, site_tensor, old_sector[:, None], new_sector[None, :])


def solution(mesh):
    placed = (P("sec", None), P("sec", "aux"), P("sec", None), P("sec"), P())
    return jax.shard_map(
        functools.partial(body, mesh.shape["sec"], mesh.shape["aux"]),
        mesh=mesh,
        in_specs=placed,
        out_specs=(P(("sec", "aux"), None), P("sec", "aux")),
        check_vma=False,
    )
```

```python
import functools

import jax
import jax.numpy as jnp
from jax import lax
from jax.experimental import pallas as pl
from jax.experimental.pallas import tpu as pltpu
from jax.sharding import PartitionSpec as P

MESH = pl.DeviceIdType.MESH
CHUNKS = 4


def tdot(a, b):
    return lax.dot_general(a, b, (((0,), (0,)), ((), ())), preferred_element_type=jnp.float32)


def kernel(
    nz, na, w_ref, d_ref, s_ref, old_ref, new_ref, sig_ref, rot_ref,
    wf, sf, df, sm, acc, img, rotacc, keep, msend, mrecv, ssend, srecv, tmp,
    loc, z_s, z_r, wr_s, wl_s, w_r, dr_s, dl_s, d_r, p_s, p_r, m_s, m_r, x_s, x_r, y_s, y_r,
):
    nc = na // 2
    z = lax.axis_index("sec")
    a = lax.axis_index("aux")
    c = lax.rem(a, 2)
    q = a // 2
    mate = a + 1 - 2 * c
    local = d_ref.shape[0]
    rows = local // na
    width = sf.shape[2]
    cols = w_ref.shape[1]
    step = cols // CHUNKS

    def peer(k):
        return lax.rem(a + 2 * k, na)

    def back(k):
        return lax.rem(a + na - 2 * k, na)

    def part(b):
        return pl.ds(pl.multiple_of(b * rows, rows), rows)

    def block(t):
        return pl.ds(pl.multiple_of(t * width, width), width)

    mine = part(a)

    loads = [
        pltpu.make_async_copy(s_ref.at[mine], sm, loc.at[0]),
        pltpu.make_async_copy(d_ref, df.at[z], loc.at[1]),
        pltpu.make_async_copy(w_ref, wf.at[z], loc.at[2]),
        pltpu.make_async_copy(s_ref.at[:, block(z)], sf.at[z], loc.at[3]),
    ]
    for load in loads:
        load.start()

    barrier = pltpu.get_barrier_semaphore()
    for k in range(1, nz):
        pl.semaphore_signal(barrier, inc=1, device_id={"sec": lax.rem(z + k, nz)}, device_id_type=MESH)
    for k in range(1, nc):
        pl.semaphore_signal(barrier, inc=1, device_id={"aux": peer(k)}, device_id_type=MESH)
    pl.semaphore_signal(barrier, inc=1, device_id={"aux": mate}, device_id_type=MESH)
    pl.semaphore_wait(barrier, nz - 1 + nc - 1 + 1)

    def remote(src, dst, send, recv, where):
        return pltpu.make_async_remote_copy(
            src_ref=src, dst_ref=dst, send_sem=send, recv_sem=recv, device_id=where, device_id_type=MESH
        )

    full = (wf, sf)

    def s_copy(k):
        t = lax.rem(z + k, nz)
        return remote(sm.at[:, block(t)], sf.at[z, mine], z_s.at[k], z_r.at[k], {"sec": t})

    def s_arrived(k):
        p = lax.rem(z + nz - k, nz)
        ref = sf.at[p, mine]
        remote(ref, ref, z_s.at[k], z_r.at[k], {"sec": p}).wait_recv()

    def p_copy(kind, p, k):
        ref = full[kind].at[p, mine]
        return remote(ref, ref, p_s.at[kind, p, k], p_r.at[kind, p, k], {"aux": peer(k)})

    def p_arrived(kind, p, k):
        ref = full[kind].at[p, part(back(k))]
        remote(ref, ref, p_s.at[kind, p, k], p_r.at[kind, p, k], {"aux": back(k)}).wait_recv()

    def m_copy(kind, p, k):
        ref = full[kind].at[p, part(back(k))]
        return remote(ref, ref, m_s.at[kind, p, k], m_r.at[kind, p, k], {"aux": mate})

    def m_arrived(kind, p, k):
        theirs = lax.rem(mate + na - 2 * k, na)
        ref = full[kind].at[p, part(theirs)]
        remote(ref, ref, m_s.at[kind, p, k], m_r.at[kind, p, k], {"aux": mate}).wait_recv()

    def spread(kind, p):
        for k in range(1, nc):
            p_copy(kind, p, k).start()
        m_copy(kind, p, 0).start()

    def relay(kind, p):
        for k in range(1, nc):
            p_arrived(kind, p, k)
            m_copy(kind, p, k).start()

    def landed(kind, p):
        for k in range(nc):
            m_arrived(kind, p, k)

    def sides(distance, act):
        @pl.when(z - distance >= 0)
        def _():
            act(z - distance)

        @pl.when(z + distance < nz)
        def _():
            act(z + distance)

    def w_right(p, src):
        return remote(src, wf.at[p, mine], wr_s.at[p], w_r.at[p], {"sec": z + 1})

    def w_left(p, src):
        return remote(src, wf.at[p, mine], wl_s.at[p], w_r.at[p], {"sec": z - 1})

    def w_step(distance):
        @pl.when(z - distance >= 0)
        def _():
            p = z - distance
            ref = wf.at[p, mine]
            remote(ref, ref, wr_s.at[p], w_r.at[p], {"sec": z - 1}).wait_recv()

            @pl.when(z < nz - 1)
            def _():
                w_right(p, ref).start()

            spread(0, p)

        @pl.when(z + distance < nz)
        def _():
            p = z + distance
            ref = wf.at[p, mine]
            remote(ref, ref, wl_s.at[p], w_r.at[p], {"sec": z + 1}).wait_recv()

            @pl.when(z > 0)
            def _():
                w_left(p, ref).start()

            spread(0, p)

    def d_right(p):
        return remote(df.at[p], df.at[p], dr_s.at[p], d_r.at[p], {"sec": z + 1})

    def d_left(p):
        return remote(df.at[p], df.at[p], dl_s.at[p], d_r.at[p], {"sec": z - 1})

    def d_step(distance):
        @pl.when(z - distance >= 0)
        def _():
            p = z - distance
            remote(df.at[p], df.at[p], dr_s.at[p], d_r.at[p], {"sec": z - 1}).wait_recv()

            @pl.when(z < nz - 1)
            def _():
                d_right(p).start()

        @pl.when(z + distance < nz)
        def _():
            p = z + distance
            remote(df.at[p], df.at[p], dl_s.at[p], d_r.at[p], {"sec": z + 1}).wait_recv()

            @pl.when(z > 0)
            def _():
                d_left(p).start()

    @pl.when(z < nz - 1)
    def _():
        w_right(z, w_ref.at[mine]).start()

    @pl.when(z > 0)
    def _():
        w_left(z, w_ref.at[mine]).start()


    loads[0].wait()
    for t in range(nz):
        band = pl.ds(t * width, width)
        offset = new_ref[:, band] - old_ref[mine, :]
        allowed = (offset >= 0) & (offset <= 2)
        sm[:, band] = jnp.where(allowed, sm[:, band].astype(jnp.float32), 0.0).astype(jnp.bfloat16)
    for k in range(1, nz):
        s_copy(k).start()
    loads[1].wait()

    @pl.when(z < nz - 1)
    def _():
        d_right(z).start()

    @pl.when(z > 0)
    def _():
        d_left(z).start()

    loads[3].wait()

    @pl.loop(0, local // 128)
    def _(i):
        r = pl.ds(pl.multiple_of(i * 128, 128), 128)
        offset = new_ref[:, block(z)] - old_ref[r, :]
        allowed = (offset >= 0) & (offset <= 2)
        sf[z, r, :] = jnp.where(allowed, sf[z, r, :].astype(jnp.float32), 0.0).astype(jnp.bfloat16)

    loads[2].wait()

    def add_images(p, first):
        @pl.loop(0, cols // 512)
        def _(i):
            r = pl.ds(pl.multiple_of(i * 512, 512), 512)
            term = tdot(df[p], wf[p, :, r])
            acc[:, r] = term if first else acc[:, r] + term

    def add_rotated(p, first):
        @pl.loop(0, width // 256)
        def _(i):
            r = pl.ds(pl.multiple_of(i * 256, 256), 256)
            term = tdot(sf[p, :, r], df[p])
            rotacc[r, :] = term if first else rotacc[r, :] + term

    add_images(z, True)
    w_step(1)
    add_rotated(z, True)
    w_step(2)
    sides(1, lambda p: relay(0, p))
    d_step(1)
    for d in range(3, nz):
        w_step(d)
    others = [lax.rem(z + nz - j, nz) for j in range(1, nz)]
    for j in range(1, nz):
        s_arrived(j)
        spread(1, others[j - 1])
    for d in range(2, nz):
        sides(d, lambda p: relay(0, p))
    for d in range(2, nz - 1):
        d_step(d)
    for p in others:
        relay(1, p)

    def images_of(p):
        landed(0, p)
        add_images(p, False)

    for d in range(1, nz - 1):
        sides(d, images_of)
    for p in others:
        landed(1, p)
    for d in range(1, nz - 1):
        sides(d, lambda p: add_rotated(p, False))
    if nz > 2:
        d_step(nz - 1)
    sides(nz - 1, lambda p: landed(0, p))

    def x_copy(i):
        r = pl.ds(i * step, step)
        return remote(msend.at[:, :, r], mrecv.at[:, :, r], x_s.at[i], x_r.at[i], {"aux": mate})

    def y_copy(i, k):
        r = pl.ds(i * step, step)
        return remote(ssend.at[k, :, r], srecv.at[k, :, r], y_s.at[i, k], y_r.at[i, k], {"aux": peer(k)})

    def terms(i):
        r = pl.ds(i * step, step)

        def last(p):
            acc[:, r] = acc[:, r] + tdot(df[p], wf[p, :, r])

        sides(nz - 1, last)
        img[:, r] = acc[:, r].astype(jnp.bfloat16)

        @pl.loop(0, nc)
        def _(b):
            pair = pl.ds(pl.multiple_of(b * 2 * rows, 2 * rows), 2 * rows)
            tmp[...] = jnp.dot(df[z, pair, :], img[:, r], preferred_element_type=jnp.float32)
            keep[b, :, r] = tmp[part(c), :]
            msend[b, :, r] = tmp[part(1 - c), :].astype(jnp.bfloat16)

        x_copy(i).start()

    def combine(i):
        r = pl.ds(i * step, step)
        x_copy(i).wait_recv()
        for k in range(1, nc):
            b = lax.rem(q + k, nc)
            ssend[k, :, r] = (keep[b, :, r] + mrecv[b, :, r].astype(jnp.float32)).astype(jnp.bfloat16)
            y_copy(i, k).start()

    for i in range(CHUNKS):
        terms(i)
        if i > 0:
            combine(i - 1)
    combine(CHUNKS - 1)

    sides(nz - 1, lambda p: add_rotated(p, False))
    rot_ref[...] = rotacc[...].astype(jnp.bfloat16)

    for i in range(CHUNKS):
        r = pl.ds(i * step, step)
        total = keep[q, :, r] + mrecv[q, :, r].astype(jnp.float32)
        for k in range(1, nc):
            y_copy(i, k).wait_recv()
            total = total + srecv[k, :, r].astype(jnp.float32)
        sig_ref[:, r] = total.astype(jnp.bfloat16)

    for j in range(1, nz):
        s_copy(j).wait_send()
        for kind in range(2):
            for k in range(1, nc):
                p_copy(kind, others[j - 1], k).wait_send()
            for k in range(nc):
                m_copy(kind, others[j - 1], k).wait_send()
    for p in range(nz):
        @pl.when((p <= z) & (z < nz - 1))
        def _():
            d_right(p).wait_send()
            w_right(p, wf.at[p, mine]).wait_send()

        @pl.when((p >= z) & (z > 0))
        def _():
            d_left(p).wait_send()
            w_left(p, wf.at[p, mine]).wait_send()
    for i in range(CHUNKS):
        x_copy(i).wait_send()
        for k in range(1, nc):
            y_copy(i, k).wait_send()


def body(nz, na, wavefunction, dressed_ops, site_tensor, old_sector, new_sector):
    local, depth = dressed_ops.shape
    cols = wavefunction.shape[1]
    width = site_tensor.shape[1] // nz
    nc, rows = na // 2, local // na
    bf, f4 = jnp.bfloat16, jnp.float32
    dma = pltpu.SemaphoreType.DMA
    vmem = pl.BlockSpec(memory_space=pltpu.VMEM)
    hbm = pl.BlockSpec(memory_space=pl.ANY)
    return pl.pallas_call(
        functools.partial(kernel, nz, na),
        out_shape=(
            jax.ShapeDtypeStruct((rows, cols), bf),
            jax.ShapeDtypeStruct((width, depth), bf),
        ),
        in_specs=[hbm, hbm, hbm, vmem, vmem],
        out_specs=(vmem, vmem),
        scratch_shapes=[
            pltpu.VMEM((nz, local, cols), bf),
            pltpu.VMEM((nz, local, width), bf),
            pltpu.VMEM((nz, local, depth), bf),
            pltpu.VMEM((rows, nz * width), bf),
            pltpu.VMEM((depth, cols), f4),
            pltpu.VMEM((depth, cols), bf),
            pltpu.VMEM((width, depth), f4),
            pltpu.VMEM((nc, rows, cols), f4),
            pltpu.VMEM((nc, rows, cols), bf),
            pltpu.VMEM((nc, rows, cols), bf),
            pltpu.VMEM((nc, rows, cols), bf),
            pltpu.VMEM((nc, rows, cols), bf),
            pltpu.VMEM((2 * rows, cols // CHUNKS), f4),
            dma((4,)),
            dma((nz,)),
            dma((nz,)),
            dma((nz,)),
            dma((nz,)),
            dma((nz,)),
            dma((nz,)),
            dma((nz,)),
            dma((nz,)),
            dma((2, nz, nc)),
            dma((2, nz, nc)),
            dma((2, nz, nc)),
            dma((2, nz, nc)),
            dma((CHUNKS,)),
            dma((CHUNKS,)),
            dma((CHUNKS, nc)),
            dma((CHUNKS, nc)),
        ],
        compiler_params=pltpu.CompilerParams(
            collective_id=0, has_side_effects=True, vmem_limit_bytes=64 * 1024 * 1024
        ),
    )(wavefunction, dressed_ops, site_tensor, old_sector[:, None], new_sector[None, :])


def solution(mesh):
    placed = (P("sec", None), P("sec", "aux"), P("sec", None), P("sec"), P())
    return jax.shard_map(
        functools.partial(body, mesh.shape["sec"], mesh.shape["aux"]),
        mesh=mesh,
        in_specs=placed,
        out_specs=(P(("sec", "aux"), None), P("sec", "aux")),
        check_vma=False,
    )
```

```python
import functools

import jax
import jax.numpy as jnp
from jax import lax
from jax.experimental import pallas as pl
from jax.experimental.pallas import tpu as pltpu
from jax.sharding import PartitionSpec as P

MESH = pl.DeviceIdType.MESH
CHUNKS = 4


def tdot(a, b):
    return lax.dot_general(a, b, (((0,), (0,)), ((), ())), preferred_element_type=jnp.float32)


def kernel(
    nz, na, w_ref, d_ref, s_ref, old_ref, new_ref, sig_ref, rot_ref,
    wf, sf, df, sm, acc, img, rotacc, keep, msend, mrecv, ssend, srecv, tmp,
    loc, z_s, z_r, wr_s, wl_s, w_r, dr_s, dl_s, d_r, p_s, p_r, m_s, m_r, x_s, x_r, y_s, y_r,
):
    nc = na // 2
    z = lax.axis_index("sec")
    a = lax.axis_index("aux")
    c = lax.rem(a, 2)
    q = a // 2
    mate = a + 1 - 2 * c
    local = d_ref.shape[0]
    rows = local // na
    width = sf.shape[2]
    cols = w_ref.shape[1]
    step = cols // CHUNKS

    def peer(k):
        return lax.rem(a + 2 * k, na)

    def back(k):
        return lax.rem(a + na - 2 * k, na)

    def part(b):
        return pl.ds(pl.multiple_of(b * rows, rows), rows)

    def block(t):
        return pl.ds(pl.multiple_of(t * width, width), width)

    mine = part(a)

    loads = [
        pltpu.make_async_copy(s_ref.at[mine], sm, loc.at[0]),
        pltpu.make_async_copy(d_ref, df.at[z], loc.at[1]),
        pltpu.make_async_copy(w_ref, wf.at[z], loc.at[2]),
        pltpu.make_async_copy(s_ref.at[:, block(z)], sf.at[z], loc.at[3]),
    ]
    for load in loads:
        load.start()

    barrier = pltpu.get_barrier_semaphore()
    for k in range(1, nz):
        pl.semaphore_signal(barrier, inc=1, device_id={"sec": lax.rem(z + k, nz)}, device_id_type=MESH)
    for k in range(1, nc):
        pl.semaphore_signal(barrier, inc=1, device_id={"aux": peer(k)}, device_id_type=MESH)
    pl.semaphore_signal(barrier, inc=1, device_id={"aux": mate}, device_id_type=MESH)
    pl.semaphore_wait(barrier, nz - 1 + nc - 1 + 1)

    def remote(src, dst, send, recv, where):
        return pltpu.make_async_remote_copy(
            src_ref=src, dst_ref=dst, send_sem=send, recv_sem=recv, device_id=where, device_id_type=MESH
        )

    full = (wf, sf)

    def s_copy(k):
        t = lax.rem(z + k, nz)
        return remote(sm.at[:, block(t)], sf.at[z, mine], z_s.at[k], z_r.at[k], {"sec": t})

    def s_arrived(k):
        p = lax.rem(z + nz - k, nz)
        ref = sf.at[p, mine]
        remote(ref, ref, z_s.at[k], z_r.at[k], {"sec": p}).wait_recv()

    def p_copy(kind, p, k):
        ref = full[kind].at[p, mine]
        return remote(ref, ref, p_s.at[kind, p, k], p_r.at[kind, p, k], {"aux": peer(k)})

    def p_arrived(kind, p, k):
        ref = full[kind].at[p, part(back(k))]
        remote(ref, ref, p_s.at[kind, p, k], p_r.at[kind, p, k], {"aux": back(k)}).wait_recv()

    def m_copy(kind, p, k):
        ref = full[kind].at[p, part(back(k))]
        return remote(ref, ref, m_s.at[kind, p, k], m_r.at[kind, p, k], {"aux": mate})

    def m_arrived(kind, p, k):
        theirs = lax.rem(mate + na - 2 * k, na)
        ref = full[kind].at[p, part(theirs)]
        remote(ref, ref, m_s.at[kind, p, k], m_r.at[kind, p, k], {"aux": mate}).wait_recv()

    def spread(kind, p):
        for k in range(1, nc):
            p_copy(kind, p, k).start()
        m_copy(kind, p, 0).start()

    def relay(kind, p):
        for k in range(1, nc):
            p_arrived(kind, p, k)
            m_copy(kind, p, k).start()

    def landed(kind, p):
        for k in range(nc):
            m_arrived(kind, p, k)

    def sides(distance, act):
        @pl.when(z - distance >= 0)
        def _():
            act(z - distance)

        @pl.when(z + distance < nz)
        def _():
            act(z + distance)

    def w_right(p, src):
        return remote(src, wf.at[p, mine], wr_s.at[p], w_r.at[p], {"sec": z + 1})

    def w_left(p, src):
        return remote(src, wf.at[p, mine], wl_s.at[p], w_r.at[p], {"sec": z - 1})

    def w_step(distance):
        @pl.when(z - distance >= 0)
        def _():
            p = z - distance
            ref = wf.at[p, mine]
            remote(ref, ref, wr_s.at[p], w_r.at[p], {"sec": z - 1}).wait_recv()

            @pl.when(z < nz - 1)
            def _():
                w_right(p, ref).start()

            spread(0, p)

        @pl.when(z + distance < nz)
        def _():
            p = z + distance
            ref = wf.at[p, mine]
            remote(ref, ref, wl_s.at[p], w_r.at[p], {"sec": z + 1}).wait_recv()

            @pl.when(z > 0)
            def _():
                w_left(p, ref).start()

            spread(0, p)

    def d_right(p):
        return remote(df.at[p], df.at[p], dr_s.at[p], d_r.at[p], {"sec": z + 1})

    def d_left(p):
        return remote(df.at[p], df.at[p], dl_s.at[p], d_r.at[p], {"sec": z - 1})

    def d_step(distance):
        @pl.when(z - distance >= 0)
        def _():
            p = z - distance
            remote(df.at[p], df.at[p], dr_s.at[p], d_r.at[p], {"sec": z - 1}).wait_recv()

            @pl.when(z < nz - 1)
            def _():
                d_right(p).start()

        @pl.when(z + distance < nz)
        def _():
            p = z + distance
            remote(df.at[p], df.at[p], dl_s.at[p], d_r.at[p], {"sec": z + 1}).wait_recv()

            @pl.when(z > 0)
            def _():
                d_left(p).start()

    @pl.when(z < nz - 1)
    def _():
        w_right(z, w_ref.at[mine]).start()

    @pl.when(z > 0)
    def _():
        w_left(z, w_ref.at[mine]).start()


    loads[0].wait()
    for t in range(nz):
        band = pl.ds(t * width, width)
        offset = new_ref[:, band] - old_ref[mine, :]
        allowed = (offset >= 0) & (offset <= 2)
        sm[:, band] = jnp.where(allowed, sm[:, band].astype(jnp.float32), 0.0).astype(jnp.bfloat16)
    for k in range(1, nz):
        s_copy(k).start()
    loads[1].wait()

    @pl.when(z < nz - 1)
    def _():
        d_right(z).start()

    @pl.when(z > 0)
    def _():
        d_left(z).start()

    loads[3].wait()

    @pl.loop(0, local // 128)
    def _(i):
        r = pl.ds(pl.multiple_of(i * 128, 128), 128)
        offset = new_ref[:, block(z)] - old_ref[r, :]
        allowed = (offset >= 0) & (offset <= 2)
        sf[z, r, :] = jnp.where(allowed, sf[z, r, :].astype(jnp.float32), 0.0).astype(jnp.bfloat16)

    loads[2].wait()

    def add_images(p, first):
        @pl.loop(0, cols // 512)
        def _(i):
            r = pl.ds(pl.multiple_of(i * 512, 512), 512)
            term = tdot(df[p], wf[p, :, r])
            acc[:, r] = term if first else acc[:, r] + term

    def add_rotated(p, first):
        @pl.loop(0, width // 256)
        def _(i):
            r = pl.ds(pl.multiple_of(i * 256, 256), 256)
            term = tdot(sf[p, :, r], df[p])
            rotacc[r, :] = term if first else rotacc[r, :] + term

    add_images(z, True)
    w_step(1)
    add_rotated(z, True)
    w_step(2)
    d_step(1)
    for d in range(3, nz):
        w_step(d)
    others = [lax.rem(z + nz - j, nz) for j in range(1, nz)]
    for j in range(1, nz):
        s_arrived(j)
        spread(1, others[j - 1])
    for d in range(2, nz - 1):
        d_step(d)
    for d in range(1, nz):
        sides(d, lambda p: relay(0, p))
    for p in others:
        relay(1, p)

    def images_of(p):
        landed(0, p)
        add_images(p, False)

    for d in range(1, nz - 1):
        sides(d, images_of)
    for p in others:
        landed(1, p)
    for d in range(1, nz - 1):
        sides(d, lambda p: add_rotated(p, False))
    if nz > 2:
        d_step(nz - 1)
    sides(nz - 1, lambda p: landed(0, p))

    def x_copy(i):
        r = pl.ds(i * step, step)
        return remote(msend.at[:, :, r], mrecv.at[:, :, r], x_s.at[i], x_r.at[i], {"aux": mate})

    def y_copy(i, k):
        r = pl.ds(i * step, step)
        return remote(ssend.at[k, :, r], srecv.at[k, :, r], y_s.at[i, k], y_r.at[i, k], {"aux": peer(k)})

    def terms(i):
        r = pl.ds(i * step, step)

        def last(p):
            acc[:, r] = acc[:, r] + tdot(df[p], wf[p, :, r])

        sides(nz - 1, last)
        img[:, r] = acc[:, r].astype(jnp.bfloat16)

        @pl.loop(0, nc)
        def _(b):
            pair = pl.ds(pl.multiple_of(b * 2 * rows, 2 * rows), 2 * rows)
            tmp[...] = jnp.dot(df[z, pair, :], img[:, r], preferred_element_type=jnp.float32)
            keep[b, :, r] = tmp[part(c), :]
            msend[b, :, r] = tmp[part(1 - c), :].astype(jnp.bfloat16)

        x_copy(i).start()

    def combine(i):
        r = pl.ds(i * step, step)
        x_copy(i).wait_recv()
        for k in range(1, nc):
            b = lax.rem(q + k, nc)
            ssend[k, :, r] = (keep[b, :, r] + mrecv[b, :, r].astype(jnp.float32)).astype(jnp.bfloat16)
            y_copy(i, k).start()

    for i in range(CHUNKS):
        terms(i)
        if i > 0:
            combine(i - 1)
    combine(CHUNKS - 1)

    sides(nz - 1, lambda p: add_rotated(p, False))
    rot_ref[...] = rotacc[...].astype(jnp.bfloat16)

    for i in range(CHUNKS):
        r = pl.ds(i * step, step)
        total = keep[q, :, r] + mrecv[q, :, r].astype(jnp.float32)
        for k in range(1, nc):
            y_copy(i, k).wait_recv()
            total = total + srecv[k, :, r].astype(jnp.float32)
        sig_ref[:, r] = total.astype(jnp.bfloat16)

    for j in range(1, nz):
        s_copy(j).wait_send()
        for kind in range(2):
            for k in range(1, nc):
                p_copy(kind, others[j - 1], k).wait_send()
            for k in range(nc):
                m_copy(kind, others[j - 1], k).wait_send()
    for p in range(nz):
        @pl.when((p <= z) & (z < nz - 1))
        def _():
            d_right(p).wait_send()
            w_right(p, wf.at[p, mine]).wait_send()

        @pl.when((p >= z) & (z > 0))
        def _():
            d_left(p).wait_send()
            w_left(p, wf.at[p, mine]).wait_send()
    for i in range(CHUNKS):
        x_copy(i).wait_send()
        for k in range(1, nc):
            y_copy(i, k).wait_send()


def body(nz, na, wavefunction, dressed_ops, site_tensor, old_sector, new_sector):
    local, depth = dressed_ops.shape
    cols = wavefunction.shape[1]
    width = site_tensor.shape[1] // nz
    nc, rows = na // 2, local // na
    bf, f4 = jnp.bfloat16, jnp.float32
    dma = pltpu.SemaphoreType.DMA
    vmem = pl.BlockSpec(memory_space=pltpu.VMEM)
    hbm = pl.BlockSpec(memory_space=pl.ANY)
    return pl.pallas_call(
        functools.partial(kernel, nz, na),
        out_shape=(
            jax.ShapeDtypeStruct((rows, cols), bf),
            jax.ShapeDtypeStruct((width, depth), bf),
        ),
        in_specs=[hbm, hbm, hbm, vmem, vmem],
        out_specs=(vmem, vmem),
        scratch_shapes=[
            pltpu.VMEM((nz, local, cols), bf),
            pltpu.VMEM((nz, local, width), bf),
            pltpu.VMEM((nz, local, depth), bf),
            pltpu.VMEM((rows, nz * width), bf),
            pltpu.VMEM((depth, cols), f4),
            pltpu.VMEM((depth, cols), bf),
            pltpu.VMEM((width, depth), f4),
            pltpu.VMEM((nc, rows, cols), f4),
            pltpu.VMEM((nc, rows, cols), bf),
            pltpu.VMEM((nc, rows, cols), bf),
            pltpu.VMEM((nc, rows, cols), bf),
            pltpu.VMEM((nc, rows, cols), bf),
            pltpu.VMEM((2 * rows, cols // CHUNKS), f4),
            dma((4,)),
            dma((nz,)),
            dma((nz,)),
            dma((nz,)),
            dma((nz,)),
            dma((nz,)),
            dma((nz,)),
            dma((nz,)),
            dma((nz,)),
            dma((2, nz, nc)),
            dma((2, nz, nc)),
            dma((2, nz, nc)),
            dma((2, nz, nc)),
            dma((CHUNKS,)),
            dma((CHUNKS,)),
            dma((CHUNKS, nc)),
            dma((CHUNKS, nc)),
        ],
        compiler_params=pltpu.CompilerParams(
            collective_id=0, has_side_effects=True, vmem_limit_bytes=64 * 1024 * 1024
        ),
    )(wavefunction, dressed_ops, site_tensor, old_sector[:, None], new_sector[None, :])


def solution(mesh):
    placed = (P("sec", None), P("sec", "aux"), P("sec", None), P("sec"), P())
    return jax.shard_map(
        functools.partial(body, mesh.shape["sec"], mesh.shape["aux"]),
        mesh=mesh,
        in_specs=placed,
        out_specs=(P(("sec", "aux"), None), P("sec", "aux")),
        check_vma=False,
    )
```

```python
import functools

import jax
import jax.numpy as jnp
from jax import lax
from jax.experimental import pallas as pl
from jax.experimental.pallas import tpu as pltpu
from jax.sharding import PartitionSpec as P

MESH = pl.DeviceIdType.MESH
CHUNKS = 4


def tdot(a, b):
    return lax.dot_general(a, b, (((0,), (0,)), ((), ())), preferred_element_type=jnp.float32)


def kernel(
    nz, na, w_ref, d_ref, s_ref, old_ref, new_ref, sig_ref, rot_ref,
    wf, sf, df, sm, acc, img, rotacc, keep, msend, mrecv, ssend, srecv, tmp,
    loc, z_s, z_r, wr_s, wl_s, w_r, dr_s, dl_s, d_r, p_s, p_r, m_s, m_r, x_s, x_r, y_s, y_r,
):
    nc = na // 2
    z = lax.axis_index("sec")
    a = lax.axis_index("aux")
    c = lax.rem(a, 2)
    q = a // 2
    mate = a + 1 - 2 * c
    local = d_ref.shape[0]
    rows = local // na
    width = sf.shape[2]
    cols = w_ref.shape[1]
    step = cols // CHUNKS

    def peer(k):
        return lax.rem(a + 2 * k, na)

    def back(k):
        return lax.rem(a + na - 2 * k, na)

    def part(b):
        return pl.ds(pl.multiple_of(b * rows, rows), rows)

    def block(t):
        return pl.ds(pl.multiple_of(t * width, width), width)

    mine = part(a)

    loads = [
        pltpu.make_async_copy(s_ref.at[mine], sm, loc.at[0]),
        pltpu.make_async_copy(d_ref, df.at[z], loc.at[1]),
        pltpu.make_async_copy(w_ref, wf.at[z], loc.at[2]),
        pltpu.make_async_copy(s_ref.at[:, block(z)], sf.at[z], loc.at[3]),
    ]
    for load in loads:
        load.start()

    barrier = pltpu.get_barrier_semaphore()
    for k in range(1, nz):
        pl.semaphore_signal(barrier, inc=1, device_id={"sec": lax.rem(z + k, nz)}, device_id_type=MESH)
    for k in range(1, nc):
        pl.semaphore_signal(barrier, inc=1, device_id={"aux": peer(k)}, device_id_type=MESH)
    pl.semaphore_signal(barrier, inc=1, device_id={"aux": mate}, device_id_type=MESH)
    pl.semaphore_wait(barrier, nz - 1 + nc - 1 + 1)

    def remote(src, dst, send, recv, where):
        return pltpu.make_async_remote_copy(
            src_ref=src, dst_ref=dst, send_sem=send, recv_sem=recv, device_id=where, device_id_type=MESH
        )

    full = (wf, sf)

    def s_copy(k):
        t = lax.rem(z + k, nz)
        return remote(sm.at[:, block(t)], sf.at[z, mine], z_s.at[k], z_r.at[k], {"sec": t})

    def s_arrived(k):
        p = lax.rem(z + nz - k, nz)
        ref = sf.at[p, mine]
        remote(ref, ref, z_s.at[k], z_r.at[k], {"sec": p}).wait_recv()

    def p_copy(kind, p, k):
        ref = full[kind].at[p, mine]
        return remote(ref, ref, p_s.at[kind, p, k], p_r.at[kind, p, k], {"aux": peer(k)})

    def p_arrived(kind, p, k):
        ref = full[kind].at[p, part(back(k))]
        remote(ref, ref, p_s.at[kind, p, k], p_r.at[kind, p, k], {"aux": back(k)}).wait_recv()

    def m_copy(kind, p, k):
        ref = full[kind].at[p, part(back(k))]
        return remote(ref, ref, m_s.at[kind, p, k], m_r.at[kind, p, k], {"aux": mate})

    def m_arrived(kind, p, k):
        theirs = lax.rem(mate + na - 2 * k, na)
        ref = full[kind].at[p, part(theirs)]
        remote(ref, ref, m_s.at[kind, p, k], m_r.at[kind, p, k], {"aux": mate}).wait_recv()

    def spread(kind, p):
        for k in range(1, nc):
            p_copy(kind, p, k).start()
        m_copy(kind, p, 0).start()

    def relay(kind, p):
        for k in range(1, nc):
            p_arrived(kind, p, k)
            m_copy(kind, p, k).start()

    def landed(kind, p):
        for k in range(nc):
            m_arrived(kind, p, k)

    def sides(distance, act):
        @pl.when(z - distance >= 0)
        def _():
            act(z - distance)

        @pl.when(z + distance < nz)
        def _():
            act(z + distance)

    def w_right(p, src):
        return remote(src, wf.at[p, mine], wr_s.at[p], w_r.at[p], {"sec": z + 1})

    def w_left(p, src):
        return remote(src, wf.at[p, mine], wl_s.at[p], w_r.at[p], {"sec": z - 1})

    def w_step(distance):
        @pl.when(z - distance >= 0)
        def _():
            p = z - distance
            ref = wf.at[p, mine]
            remote(ref, ref, wr_s.at[p], w_r.at[p], {"sec": z - 1}).wait_recv()

            @pl.when(z < nz - 1)
            def _():
                w_right(p, ref).start()

            spread(0, p)

        @pl.when(z + distance < nz)
        def _():
            p = z + distance
            ref = wf.at[p, mine]
            remote(ref, ref, wl_s.at[p], w_r.at[p], {"sec": z + 1}).wait_recv()

            @pl.when(z > 0)
            def _():
                w_left(p, ref).start()

            spread(0, p)

    def d_right(p, src=None):
        return remote(df.at[p] if src is None else src, df.at[p], dr_s.at[p], d_r.at[p], {"sec": z + 1})

    def d_left(p, src=None):
        return remote(df.at[p] if src is None else src, df.at[p], dl_s.at[p], d_r.at[p], {"sec": z - 1})

    def d_step(distance):
        @pl.when(z - distance >= 0)
        def _():
            p = z - distance
            remote(df.at[p], df.at[p], dr_s.at[p], d_r.at[p], {"sec": z - 1}).wait_recv()

            @pl.when(z < nz - 1)
            def _():
                d_right(p).start()

        @pl.when(z + distance < nz)
        def _():
            p = z + distance
            remote(df.at[p], df.at[p], dl_s.at[p], d_r.at[p], {"sec": z + 1}).wait_recv()

            @pl.when(z > 0)
            def _():
                d_left(p).start()

    @pl.when(z < nz - 1)
    def _():
        w_right(z, w_ref.at[mine]).start()

    @pl.when(z > 0)
    def _():
        w_left(z, w_ref.at[mine]).start()


    loads[0].wait()
    for t in range(nz):
        band = pl.ds(t * width, width)
        offset = new_ref[:, band] - old_ref[mine, :]
        allowed = (offset >= 0) & (offset <= 2)
        sm[:, band] = jnp.where(allowed, sm[:, band].astype(jnp.float32), 0.0).astype(jnp.bfloat16)
    loads[3].wait()

    @pl.loop(0, local // 128)
    def _(i):
        r = pl.ds(pl.multiple_of(i * 128, 128), 128)
        offset = new_ref[:, block(z)] - old_ref[r, :]
        allowed = (offset >= 0) & (offset <= 2)
        sf[z, r, :] = jnp.where(allowed, sf[z, r, :].astype(jnp.float32), 0.0).astype(jnp.bfloat16)

    loads[2].wait()

    def add_images(p, first):
        @pl.loop(0, cols // 512)
        def _(i):
            r = pl.ds(pl.multiple_of(i * 512, 512), 512)
            term = tdot(df[p], wf[p, :, r])
            acc[:, r] = term if first else acc[:, r] + term

    def add_rotated(p, first):
        @pl.loop(0, width // 256)
        def _(i):
            r = pl.ds(pl.multiple_of(i * 256, 256), 256)
            term = tdot(sf[p, :, r], df[p])
            rotacc[r, :] = term if first else rotacc[r, :] + term

    w_step(1)
    for d in range(2, nz - 1):
        w_step(d)
    @pl.when(z < nz - 1)
    def _():
        d_right(z, d_ref).start()

    @pl.when(z > 0)
    def _():
        d_left(z, d_ref).start()

    for k in range(1, nz):
        s_copy(k).start()
    loads[1].wait()
    add_images(z, True)
    add_rotated(z, True)
    d_step(1)
    for d in range(max(2, nz - 1), nz):
        w_step(d)
    others = [lax.rem(z + nz - j, nz) for j in range(1, nz)]
    for j in range(1, nz):
        s_arrived(j)
        spread(1, others[j - 1])
    for d in range(2, nz - 1):
        d_step(d)
    for d in range(1, nz):
        sides(d, lambda p: relay(0, p))
    for p in others:
        relay(1, p)

    def images_of(p):
        landed(0, p)
        add_images(p, False)

    for d in range(1, nz - 1):
        sides(d, images_of)
    for p in others:
        landed(1, p)
    for d in range(1, nz - 1):
        sides(d, lambda p: add_rotated(p, False))
    if nz > 2:
        d_step(nz - 1)
    sides(nz - 1, lambda p: landed(0, p))

    def x_copy(i):
        r = pl.ds(i * step, step)
        return remote(msend.at[:, :, r], mrecv.at[:, :, r], x_s.at[i], x_r.at[i], {"aux": mate})

    def y_copy(i, k):
        r = pl.ds(i * step, step)
        return remote(ssend.at[k, :, r], srecv.at[k, :, r], y_s.at[i, k], y_r.at[i, k], {"aux": peer(k)})

    def terms(i):
        r = pl.ds(i * step, step)

        def last(p):
            acc[:, r] = acc[:, r] + tdot(df[p], wf[p, :, r])

        sides(nz - 1, last)
        img[:, r] = acc[:, r].astype(jnp.bfloat16)

        @pl.loop(0, nc)
        def _(b):
            pair = pl.ds(pl.multiple_of(b * 2 * rows, 2 * rows), 2 * rows)
            tmp[...] = jnp.dot(df[z, pair, :], img[:, r], preferred_element_type=jnp.float32)
            keep[b, :, r] = tmp[part(c), :]
            msend[b, :, r] = tmp[part(1 - c), :].astype(jnp.bfloat16)

        x_copy(i).start()

    def combine(i):
        r = pl.ds(i * step, step)
        x_copy(i).wait_recv()
        for k in range(1, nc):
            b = lax.rem(q + k, nc)
            ssend[k, :, r] = (keep[b, :, r] + mrecv[b, :, r].astype(jnp.float32)).astype(jnp.bfloat16)
            y_copy(i, k).start()

    for i in range(CHUNKS):
        terms(i)
        if i > 0:
            combine(i - 1)
    combine(CHUNKS - 1)

    sides(nz - 1, lambda p: add_rotated(p, False))
    rot_ref[...] = rotacc[...].astype(jnp.bfloat16)

    for i in range(CHUNKS):
        r = pl.ds(i * step, step)
        total = keep[q, :, r] + mrecv[q, :, r].astype(jnp.float32)
        for k in range(1, nc):
            y_copy(i, k).wait_recv()
            total = total + srecv[k, :, r].astype(jnp.float32)
        sig_ref[:, r] = total.astype(jnp.bfloat16)

    for j in range(1, nz):
        s_copy(j).wait_send()
        for kind in range(2):
            for k in range(1, nc):
                p_copy(kind, others[j - 1], k).wait_send()
            for k in range(nc):
                m_copy(kind, others[j - 1], k).wait_send()
    for p in range(nz):
        @pl.when((p <= z) & (z < nz - 1))
        def _():
            d_right(p).wait_send()
            w_right(p, wf.at[p, mine]).wait_send()

        @pl.when((p >= z) & (z > 0))
        def _():
            d_left(p).wait_send()
            w_left(p, wf.at[p, mine]).wait_send()
    for i in range(CHUNKS):
        x_copy(i).wait_send()
        for k in range(1, nc):
            y_copy(i, k).wait_send()


def body(nz, na, wavefunction, dressed_ops, site_tensor, old_sector, new_sector):
    local, depth = dressed_ops.shape
    cols = wavefunction.shape[1]
    width = site_tensor.shape[1] // nz
    nc, rows = na // 2, local // na
    bf, f4 = jnp.bfloat16, jnp.float32
    dma = pltpu.SemaphoreType.DMA
    vmem = pl.BlockSpec(memory_space=pltpu.VMEM)
    hbm = pl.BlockSpec(memory_space=pl.ANY)
    return pl.pallas_call(
        functools.partial(kernel, nz, na),
        out_shape=(
            jax.ShapeDtypeStruct((rows, cols), bf),
            jax.ShapeDtypeStruct((width, depth), bf),
        ),
        in_specs=[hbm, hbm, hbm, vmem, vmem],
        out_specs=(vmem, vmem),
        scratch_shapes=[
            pltpu.VMEM((nz, local, cols), bf),
            pltpu.VMEM((nz, local, width), bf),
            pltpu.VMEM((nz, local, depth), bf),
            pltpu.VMEM((rows, nz * width), bf),
            pltpu.VMEM((depth, cols), f4),
            pltpu.VMEM((depth, cols), bf),
            pltpu.VMEM((width, depth), f4),
            pltpu.VMEM((nc, rows, cols), f4),
            pltpu.VMEM((nc, rows, cols), bf),
            pltpu.VMEM((nc, rows, cols), bf),
            pltpu.VMEM((nc, rows, cols), bf),
            pltpu.VMEM((nc, rows, cols), bf),
            pltpu.VMEM((2 * rows, cols // CHUNKS), f4),
            dma((4,)),
            dma((nz,)),
            dma((nz,)),
            dma((nz,)),
            dma((nz,)),
            dma((nz,)),
            dma((nz,)),
            dma((nz,)),
            dma((nz,)),
            dma((2, nz, nc)),
            dma((2, nz, nc)),
            dma((2, nz, nc)),
            dma((2, nz, nc)),
            dma((CHUNKS,)),
            dma((CHUNKS,)),
            dma((CHUNKS, nc)),
            dma((CHUNKS, nc)),
        ],
        compiler_params=pltpu.CompilerParams(
            collective_id=0, has_side_effects=True, vmem_limit_bytes=64 * 1024 * 1024
        ),
    )(wavefunction, dressed_ops, site_tensor, old_sector[:, None], new_sector[None, :])


def solution(mesh):
    placed = (P("sec", None), P("sec", "aux"), P("sec", None), P("sec"), P())
    return jax.shard_map(
        functools.partial(body, mesh.shape["sec"], mesh.shape["aux"]),
        mesh=mesh,
        in_specs=placed,
        out_specs=(P(("sec", "aux"), None), P("sec", "aux")),
        check_vma=False,
    )
```
